128 devices in a mesh: row: 8 (over x, core), col: 16 (over z, y).
Axes of the slice: x: 4, y: 4, z: 4, core: 2. Of those that a mesh axis runs over, the one named last changes fastest.
Arguments:
- blocks: bfloat16 [16, 1024, 4096], P('row', 'col'), may hold values from -6 to 6
- block_atom: int32 [16, 16], P('row', 'col'), may hold values from 0 to 127, as said below
- block_pair: int32 [16, 16], P('row', 'col'), may hold values from 0 to 8, as said below
- atom_sizes: int32 [128], replicated, may hold values from 32 to 64
- density: bfloat16 [8192, 8192], P('col', 'row'), may hold values from -0.125 to 0.125
- density_pattern: int32 [128, 128], P('col', 'row'), may hold values 0 or 1
Outputs:
- contracted: bfloat16 [8, 8192, 4096], P('row', 'col')
The draws below stay inside these ranges and needn't reach their ends.
Inputs may be any that keep to these rules, and one draw needn't show every extreme that they name: `block_pair`: empty slots hold 8. The slots of one device name any one target row at most 1 times, and all slots with the same col index name any one target row at most 2 times; both bounds are reached in every draw. `block_atom`: A block in col index c has an atom of c * 8 to (c + 1) * 8 - 1; no two present blocks share both atom and pair.
All inputs are finite; a program needn't handle non-finite values. No bound on the sum of `density_pattern` on one device may be relied on, other than what follows from the above.
Results may differ from the reference program's by a relative error of at most 0.001.
Values may be sent and summed in bfloat16 or wider, within the bound.
No kernel may reach another device: no remote copies, remote signals or barrier semaphores. Data moves between devices by JAX's collectives and lax.ppermute only.
A program may use at most 128 MiB of HBM per device.

```python
import jax
import jax.numpy as jnp
from jax import lax

B = 64
LAM_DEV = 8
K_SRC = 2
SEND_CAP = 1
NATOM = 128
NORB = 8192
NPAIR = 8
GRID_COLS = 16
TILE = 4096
ROWS_SRC = 16
SLOTS = 32


def route_table(key):
    key_list = jax.random.split(key, 5)
    lead_shift = jax.random.randint(key_list[0], (GRID_COLS,), 0, NPAIR)
    other_shift = (lead_shift + 1 + jax.random.randint(key_list[1], (GRID_COLS,), 0, NPAIR - 1)) % NPAIR
    full_row = jax.random.randint(key_list[2], (GRID_COLS,), 0, NPAIR)
    source_row = jnp.arange(NPAIR, dtype=jnp.int32)[:, None, None]
    slot_index = jnp.arange(K_SRC, dtype=jnp.int32)[None, :, None]
    shifts = jnp.where(slot_index < SEND_CAP, lead_shift[None, None, :], other_shift[None, None, :])
    targets = (source_row + shifts) % NPAIR
    keeping = jax.random.randint(key_list[3], targets.shape, 0, 4) < 3
    keeping = keeping | (targets == full_row[None, None, :])
    scores = jax.random.randint(key_list[4], (NPAIR, GRID_COLS, LAM_DEV), 0, 1 << 20) * LAM_DEV + jnp.arange(LAM_DEV, dtype=jnp.int32)
    ranking = jnp.argsort(scores, axis=2).astype(jnp.int32)
    col_index = jnp.broadcast_to(jnp.arange(GRID_COLS, dtype=jnp.int32)[None, None, :], targets.shape)
    slot_all = jnp.broadcast_to(slot_index, targets.shape)
    atom_ids = col_index * LAM_DEV + ranking[targets, col_index, slot_all]
    pair_ids = jnp.where(keeping, targets, NPAIR)
    return (pair_ids.reshape(NPAIR * K_SRC, GRID_COLS).astype(jnp.int32), atom_ids.reshape(NPAIR * K_SRC, GRID_COLS).astype(jnp.int32))


def draw_block_pair(key, part):
    table = route_table(key)
    return table[0]


def draw_block_atom(key, part):
    table = route_table(key)
    return table[1]


def plant(array, stream_key, smallest, high):
    longest = array.shape.index(max(array.shape))
    spots = []
    for shift in (0, 1):
        where = [jax.random.randint(jax.random.fold_in(stream_key, axis), (), 0, length) for axis, length in enumerate(array.shape)]
        where[longest] = (where[longest] + shift) % array.shape[longest]
        spots.append(tuple(where))
    return array.at[spots[0]].set(smallest).at[spots[1]].set(high)


def levels(own_key, extent, shards, least, top_value):
    def one(position, parts):
        heights = jax.random.uniform(jax.random.fold_in(jax.random.fold_in(own_key, 6), position), (parts,), jnp.float32, least / len(shards), top_value / len(shards))
        return jnp.repeat(jnp.exp(heights), extent[position] // parts).reshape((-1,) + (1,) * (len(extent) - position - 1))

    level = one(*shards[0])
    for cut in shards[1:]:
        level = level * one(*cut)
    return level


def normal_values(own_key, shape, deviation, most, pieces=(), kind=jnp.bfloat16):
    result = jax.random.normal(own_key, shape, jnp.float32) * deviation
    if len(pieces) > 0:
        result = levels(own_key, shape, pieces, -0.22, 0.18) * result
    return jnp.clip(result, min=-most, max=most).astype(kind)


def setup_inputs(seed: int = 0) -> dict:
    seeds = jax.random.split(jax.random.key(seed), 7)
    blocks = normal_values(seeds[0], (ROWS_SRC, GRID_COLS * B, TILE), 1.0, 6.0, ((0, 8), (1, 16)))
    block_atom = draw_block_atom(jax.random.fold_in(seeds[6], 71), 0)
    block_pair = draw_block_pair(jax.random.fold_in(seeds[6], 71), 0)
    atom_sizes = plant(jax.random.randint(seeds[3], (NATOM,), B // 2, B + 1), jax.random.fold_in(seeds[3], 1), B // 2, B).astype(jnp.int32)
    density = normal_values(seeds[4], (NORB, NORB), (SLOTS * B) ** -0.5, 0.125, ((0, 16), (1, 8)))
    density_pattern = plant((jax.random.randint(seeds[5], (NATOM, NATOM), 0, 4) < 3).astype(jnp.int32), jax.random.fold_in(seeds[5], 1), 0, 1)
    return dict(blocks=blocks, block_atom=block_atom, block_pair=block_pair, atom_sizes=atom_sizes, density=density, density_pattern=density_pattern)


def reference(blocks, block_atom, block_pair, atom_sizes, density, density_pattern):
    atom_count = atom_sizes.shape[0]
    offsets = jnp.arange(B, dtype=jnp.int32)
    inside = (offsets[None, :] < atom_sizes[:, None]).astype(jnp.bfloat16)
    pattern = density_pattern.astype(jnp.bfloat16)
    factor = pattern[:, None, :, None] * inside[:, :, None, None] * inside[None, None, :, :]
    masked = (density.reshape(atom_count, B, atom_count, B) * factor).reshape(atom_count * B, atom_count, B)
    tile_list = blocks.reshape(-1, B, blocks.shape[-1])
    atom_list = block_atom.reshape(-1).astype(jnp.int32)
    pair_list = block_pair.reshape(-1).astype(jnp.int32)

    def one_pair(pair_index):
        outside = (pair_list != pair_index).astype(jnp.int32)
        ordering = jnp.argsort(outside, stable=True)[:SLOTS].astype(jnp.int32)
        present = (jnp.take(pair_list, ordering) == pair_index).astype(jnp.bfloat16)
        chosen = jnp.take(masked, jnp.take(atom_list, ordering), axis=1) * present[None, :, None]
        left_side = chosen.reshape(chosen.shape[0], -1)
        right_side = jnp.take(tile_list, ordering, axis=0).reshape(-1, blocks.shape[-1])
        return jnp.dot(left_side, right_side, preferred_element_type=jnp.float32).astype(jnp.bfloat16)

    return lax.map(one_pair, jnp.arange(NPAIR, dtype=jnp.int32))
```

```python
import jax
import jax.numpy as jnp
from jax import lax
from jax.experimental import pallas as pl
from jax.experimental.pallas import tpu as pltpu
from jax.sharding import PartitionSpec as P

FIRST = 1024
BN = 512
ORDER = (0, -1, 1, 2)
VMEM = 20 * 1024 * 1024
BESIDE = 128


def shift_row_x(v, d):
    return lax.ppermute(v, "row", [(2 * x + k, 2 * ((x + d) % 4) + k) for x in range(4) for k in range(2)])


def swap_core(v):
    return lax.ppermute(v, "row", [(r, r ^ 1) for r in range(8)])


def shift_z(v, d):
    return lax.ppermute(v, "col", [(4 * z + y, 4 * ((z + d) % 4) + y) for z in range(4) for y in range(4)])


def shift_y(v, d):
    return lax.ppermute(v, "col", [(4 * z + y, 4 * z + (y + d) % 4) for z in range(4) for y in range(4)])


def after(values):
    return lax.optimization_barrier(values)


def around(v, shift):
    return jnp.concatenate([v, shift(v, 1), shift(v, -1), shift(v, 2)], axis=0)


def relay(v, shift):
    half = v.shape[0] // 2
    minus, plus = shift(v, 1), shift(v, -1)
    return [v, minus, plus, jnp.concatenate([shift(minus[:half], 1), shift(plus[half:], -1)], axis=0)]


def spread_names(v, shift, place):
    slots = jnp.arange(4, dtype=jnp.int32).reshape((4,) + (1,) * v.ndim)
    total = jnp.where(slots == place, v[None], 0)
    for d in (1, -1, 2):
        total = total + jnp.where(slots == (place - d) % 4, shift(v, d)[None], 0)
    return total


def choose_kernel(density_ref, row_ref, pattern_ref, inside_ref, out_ref):
    rows = density_ref.shape[1]
    hit = lax.broadcasted_iota(jnp.int32, (rows, row_ref.shape[1]), 0) == row_ref[...]
    picked = jnp.dot(density_ref[...], hit.astype(jnp.bfloat16), preferred_element_type=jnp.float32)
    factor = jnp.dot(inside_ref[...], pattern_ref[...], preferred_element_type=jnp.float32)
    out_ref[0] = (picked * factor).astype(jnp.bfloat16)


def choose_columns(density, rows, pattern, inside):
    count = rows.shape[1] // 256
    m, width = density.shape
    return pl.pallas_call(
        choose_kernel,
        grid=(count,),
        in_specs=[
            pl.BlockSpec((m, width), lambda t: (0, 0)),
            pl.BlockSpec((1, 256), lambda t: (0, t)),
            pl.BlockSpec((pattern.shape[0], 256), lambda t: (0, t)),
            pl.BlockSpec(inside.shape, lambda t: (0, 0)),
        ],
        out_specs=pl.BlockSpec((1, m, 256), lambda t: (t, 0, 0)),
        out_shape=jax.ShapeDtypeStruct((count, m, 256), jnp.bfloat16),
        compiler_params=pltpu.CompilerParams(vmem_limit_bytes=VMEM),
        cost_estimate=pl.CostEstimate(
            flops=2 * m * width * rows.shape[1], bytes_accessed=2 * m * (width + rows.shape[1]), transcendentals=0
        ),
        name="choose_columns",
    )(density, rows, pattern, inside)


def order_kernel(place_ref, half_ref, *refs):
    own, other, (left1, left2) = refs[:4], refs[4], refs[5:]
    for i in range(16):
        place = place_ref[i]
        columns = pl.ds(pl.multiple_of(half_ref[i] * 128, 128), 128)
        j = (i % 4) * 4 + i // 4

        def put(block):
            left1[:, i * 128 : (i + 1) * 128] = block
            left2[:, j * 128 : (j + 1) * 128] = block

        for d in range(4):

            @pl.when(place == d)
            def _():
                put(own[d][0, :, columns])

        @pl.when(place >= 4)
        def _():
            put(other[jnp.maximum(place - 4, 0), :, columns])


def order_columns(place, half, own, other):
    m = other.shape[1]
    return pl.pallas_call(
        order_kernel,
        grid_spec=pltpu.PrefetchScalarGridSpec(
            num_scalar_prefetch=2,
            grid=(1,),
            in_specs=[pl.BlockSpec((1, m, 256), lambda i, p, h: (0, 0, 0))] * 4
            + [pl.BlockSpec(other.shape, lambda i, p, h: (0, 0, 0))],
            out_specs=[pl.BlockSpec((m, 2048), lambda i, p, h: (0, 0))] * 2,
        ),
        out_shape=[jax.ShapeDtypeStruct((m, 2048), jnp.bfloat16)] * 2,
        compiler_params=pltpu.CompilerParams(vmem_limit_bytes=VMEM),
        cost_estimate=pl.CostEstimate(flops=0, bytes_accessed=4 * 2 * m * 2048, transcendentals=0),
        name="order_columns",
    )(place, half, *own, other)


def sort_kernel(where_ref, *refs):
    names, pieces, outs = refs[:4], refs[4:8], refs[8:]
    b = outs[0].shape[1]
    spots = []
    for i, d in enumerate(ORDER):
        x = lax.rem(where_ref[2] + (d + 4), 4)
        for s in range(2):
            pair = jnp.tile(names[i][s, :1, :].astype(jnp.float32), (1, outs[0].shape[2] // BESIDE))
            spots.append((2 * x + s, pair, pieces[i][s, :b, :]))
    flip = where_ref[3] == 1
    for out, row in ((outs[0], where_ref[0]), (outs[1], where_ref[1])):
        row = row.astype(jnp.float32)
        match = [(pair == row).astype(jnp.float32) for _, pair, _ in spots]
        totals = [jnp.zeros(out.shape[1:], out.dtype), jnp.zeros(out.shape[1:], out.dtype)]
        for i, (at, _, tile) in enumerate(spots):
            before = sum(jnp.where(spots[j][0] < at, match[j], 0.0) for j in range(8) if j != i)
            first = match[i] * (1.0 - jnp.minimum(before, 1.0))
            second = match[i] * jnp.minimum(before, 1.0)
            for s, one in enumerate((jnp.where(flip, second, first), jnp.where(flip, first, second))):
                totals[s] = totals[s] + tile * one.astype(out.dtype)
        for s in range(2):
            out[s] = totals[s]


def sort_tiles(where, named, pieces):
    b, n, step = named[0].shape[1], pieces[0].shape[2], 256
    n -= BESIDE
    at = named[0].shape[2] // BESIDE - 1
    return pl.pallas_call(
        sort_kernel,
        grid_spec=pltpu.PrefetchScalarGridSpec(
            num_scalar_prefetch=1,
            grid=(n // step,),
            in_specs=[pl.BlockSpec((2, 16, BESIDE), lambda i, p: (0, 0, at))] * 4
            + [pl.BlockSpec((2, b, step), lambda i, p: (0, 0, i))] * 4,
            out_specs=[pl.BlockSpec((2, b, step), lambda i, p: (0, 0, i))] * 2,
        ),
        out_shape=[jax.ShapeDtypeStruct((2, b, n), jnp.bfloat16)] * 2,
        compiler_params=pltpu.CompilerParams(vmem_limit_bytes=VMEM),
        cost_estimate=pl.CostEstimate(flops=0, bytes_accessed=24 * b * n, transcendentals=0),
        name="sort_tiles",
    )(where, *named, *pieces)


def product_kernel(at, count, started, left_ref, *refs):
    total = refs[count][...] if started else None
    for piece in refs[:count]:
        depth = piece.shape[0] * piece.shape[1]
        right = piece[...].reshape(depth, piece.shape[2])
        term = jnp.dot(left_ref[:, at : at + depth], right, preferred_element_type=jnp.float32)
        total = term if total is None else total + term
        at += depth
    refs[-1][...] = total.astype(refs[-1].dtype)


def product(left, at, pieces, total=None, out=None, column=0, width=None):
    m = left.shape[0]
    n = pieces[0].shape[2]
    depth = sum(p.shape[0] * p.shape[1] for p in pieces)
    first = column // BN
    specs = [pl.BlockSpec(left.shape, lambda i: (0, 0))]
    specs += [pl.BlockSpec(p.shape[:2] + (BN,), lambda i: (0, 0, i)) for p in pieces]
    operands = [left, *pieces]
    if total is not None:
        specs.append(pl.BlockSpec((m, BN), lambda i: (0, i)))
        operands.append(total)
    alias = {}
    if out is not None:
        specs.append(pl.BlockSpec(memory_space=pl.ANY))
        alias = {len(operands): 0}
        operands.append(out)

    def kernel(*refs):
        product_kernel(at, len(pieces), total is not None, *refs)

    shape = jax.ShapeDtypeStruct((m, n), jnp.float32) if width is None else jax.ShapeDtypeStruct((m, width), jnp.bfloat16)
    return pl.pallas_call(
        kernel,
        grid=(n // BN,),
        in_specs=specs,
        out_specs=pl.BlockSpec((m, BN), lambda i: (0, first + i)),
        out_shape=shape,
        input_output_aliases=alias,
        compiler_params=pltpu.CompilerParams(vmem_limit_bytes=VMEM),
        cost_estimate=pl.CostEstimate(
            flops=2 * m * depth * n, bytes_accessed=2 * (left.size + (depth + 2 * m) * n), transcendentals=0
        ),
        name="product",
    )(*operands)


def per_device(blocks, block_atom, block_pair, atom_sizes, density, density_pattern):
    b, width = blocks.shape[1], blocks.shape[2]
    r, c = lax.axis_index("row"), lax.axis_index("col")
    x, k, z, y = r // 2, r % 2, c // 4, c % 4
    i32 = jnp.int32
    offsets = jnp.array(ORDER, dtype=i32)

    names = jnp.concatenate([block_pair, block_atom], axis=1)
    row_names = spread_names(spread_names(names, shift_z, z), shift_y, y)

    def beside(v):
        v = jnp.broadcast_to(v, (2,) + v.shape[-2:]).transpose(0, 2, 1).astype(jnp.bfloat16)
        v = jnp.broadcast_to(v[..., None], v.shape + (b // 2 // v.shape[2],)).reshape(2, b, 1)
        return jnp.broadcast_to(v, (2, b, BESIDE))

    start = jnp.concatenate([blocks[:, :, :FIRST], beside(names[:, None, :])], axis=2)
    where = jnp.stack([r, r + 1 - 2 * k, x, k]).astype(i32)
    near = relay(start, shift_row_x)
    mine, theirs = sort_tiles(where, near, near)
    part1 = mine + swap_core(theirs)
    table = row_names.transpose(1, 0, 2, 3).reshape(32, 2)
    rest = jnp.concatenate([blocks[:, :, FIRST:], beside(table)], axis=2)
    rest, mine, theirs = after((rest, mine, theirs))
    part1 = mine + swap_core(theirs)
    near2 = relay(rest, shift_row_x)
    mine, theirs = sort_tiles(where, near, near2)
    part2 = mine + swap_core(theirs)

    far = jnp.arange(4, dtype=i32)
    from_x = (x + offsets) % 4
    found = jnp.stack([piece[0, :, width - FIRST] for piece in near2]).astype(i32).reshape(4, 2, 32)
    found = found[:, 0] * 256 + found[:, 1]
    found = jnp.sum(jnp.where(far[:, None, None] == from_x[:, None], found, 0), axis=1).reshape(4, 16, 2)
    found2 = swap_core(found)
    code = jnp.where(k == 0, jnp.stack([found, found2], 1), jnp.stack([found2, found], 1))
    code = code.transpose(2, 0, 1, 3)

    def slots_of(code, pair):
        spot = 4 * jnp.arange(4, dtype=i32)[:, None] + jnp.arange(2, dtype=i32)
        lows, highs = [], []
        for core in range(2):
            match = (code[..., core, :] // 256) == pair[..., None, None]
            low = jnp.min(jnp.where(match, spot, 99), axis=(-2, -1))
            high = jnp.max(jnp.where(match, spot, -1), axis=(-2, -1))
            lows.append(jnp.where(low < 99, low + 2 * core, -1))
            highs.append(jnp.where(high > low, high + 2 * core, -1))
        return jnp.stack([jnp.where(lows[0] >= 0, lows[0], highs[1]), jnp.where(lows[1] >= 0, lows[1], highs[0])], -1)

    two = lax.dynamic_slice_in_dim(code, 2 * r, 2)
    pairs = (2 * ((x + far) % 4)[:, None] + (k + jnp.arange(2, dtype=i32)) % 2).reshape(8)
    source = slots_of(two[None], jnp.broadcast_to(pairs[:, None], (8, 2)))
    hit = source[..., None] == jnp.arange(16, dtype=i32)
    atom = jnp.sum(jnp.where(hit, (two % 256).reshape(2, 1, 16), 0), axis=-1)
    atom = jnp.where(source >= 0, atom - 16 * r, -1).reshape(1, 32)
    sizes_here = lax.dynamic_slice_in_dim(atom_sizes, 16 * r, 16)
    pattern_hit = jnp.arange(16, dtype=i32)[:, None] == atom
    size = jnp.sum(jnp.where(pattern_hit, sizes_here[:, None], 0), axis=0)[:, None]
    unit = jnp.arange(b, dtype=i32)
    columns = atom.reshape(32, 1)
    rows = jnp.where((unit < size) & (columns >= 0), columns * b + unit, -1).reshape(1, 32 * b)
    chosen_pattern = jnp.sum(jnp.where(pattern_hit, density_pattern[:, :, None], 0), axis=1)
    chosen_pattern = jnp.broadcast_to(chosen_pattern[:, :, None], (8, 32, b)).reshape(8, 32 * b)
    lam_sizes = lax.dynamic_slice_in_dim(atom_sizes, 8 * c, 8)
    lam = jnp.arange(8 * b, dtype=i32)[:, None]
    inside = (lam // b == jnp.arange(8, dtype=i32)) & (lam % b < lam_sizes[None, :])
    chosen = choose_columns(density, rows, chosen_pattern.astype(jnp.bfloat16), inside.astype(jnp.bfloat16))
    chosen = chosen.reshape(4, 2, 8 * b, 4 * b)
    own = [chosen[0]] + [shift_row_x(chosen[d], d) for d in (1, 2, 3)]
    other = swap_core(jnp.stack([piece[1] for piece in own]))

    from_y = jnp.repeat((y + offsets) % 4, 4)
    from_z = jnp.tile((z + offsets) % 4, 4)
    place = (x - from_z) % 4 + jnp.where(from_y // 2 == k, 0, 4)
    left1, left2 = order_columns(place.astype(i32), (from_y % 2).astype(i32), own, other)

    def spread(part, how):
        half = part.shape[2] // 2
        return how(part[:, :, :half], shift_z), how(part[:, :, half:], shift_y)

    def relay_joined(v, shift):
        return jnp.concatenate(relay(v, shift), axis=0)

    def send(g1, g2):
        return (shift_y(g1, 1), shift_y(g1, -1)), (shift_z(g2, 1), shift_z(g2, -1))

    def forward(sides):
        (minus1, plus1), (minus2, plus2) = sides
        return (
            [shift_y(minus1[:4], 1), shift_y(plus1[4:], -1)],
            [shift_z(minus2[:4], 1), shift_z(plus2[4:], -1)],
        )

    def multiply(g, sides, last, out, at):
        half = g[0].shape[2]
        totals = [product(left, 0, [v, *pair]) for left, v, pair in zip((left1, left2), g, sides)]
        for left, total, pieces in zip((left1, left2), totals, last):
            out = product(left, 24 * b, pieces, total, out, at, width)
            at += half
        return out

    g = spread(part1, around)
    sides = send(*g)
    last = forward(sides)
    part2, last = after((part2, last))
    h = spread(part2, relay_joined)
    h, _ = after((h, own))
    sides2 = send(*h)
    out = multiply(g, sides, last, None, 0)
    sides2, out = after((sides2, out))
    out = multiply(h, sides2, forward(sides2), out, FIRST)
    return out[None]


def solution(mesh):
    placed = (
        P("row", "col", None),
        P("row", "col"),
        P("row", "col"),
        P(),
        P("col", "row"),
        P("col", "row"),
    )
    return jax.shard_map(
        per_device, mesh=mesh, in_specs=placed, out_specs=P("row", "col", None), check_vma=False
    )
```

```python
import jax
import jax.numpy as jnp
from jax import lax
from jax.experimental import pallas as pl
from jax.experimental.pallas import tpu as pltpu
from jax.sharding import PartitionSpec as P

ORDER = (0, -1, 1, 2)
VMEM = 14 * 1024 * 1024
BESIDE = 128
WEIGHT = 2
PARAMS = pltpu.CompilerParams(vmem_limit_bytes=VMEM)
ANY = pl.BlockSpec(memory_space=pl.ANY)


def shift_row_x(v, d):
    return lax.ppermute(v, "row", [(2 * x + k, 2 * ((x + d) % 4) + k) for x in range(4) for k in range(2)])


def swap_core(v):
    return lax.ppermute(v, "row", [(r, r ^ 1) for r in range(8)])


def shift_z(v, d):
    return lax.ppermute(v, "col", [(4 * z + y, 4 * ((z + d) % 4) + y) for z in range(4) for y in range(4)])


def shift_y(v, d):
    return lax.ppermute(v, "col", [(4 * z + y, 4 * z + (y + d) % 4) for z in range(4) for y in range(4)])


def halves(minus, plus, others=()):
    count, b, n = minus.shape
    half, step = count // 2, min(n, 1024)

    def kernel(*refs):
        refs[-2][...] = refs[0][...]
        refs[-1][...] = refs[1][...]

    spec = pl.BlockSpec((half, b, step), lambda i: (0, 0, i))
    return pl.pallas_call(
        kernel,
        grid=(n // step,),
        in_specs=[spec, pl.BlockSpec((half, b, step), lambda i: (1, 0, i))] + [ANY] * len(others),
        out_specs=[spec, spec],
        out_shape=[jax.ShapeDtypeStruct((half, b, n), jnp.bfloat16)] * 2,
        compiler_params=PARAMS,
        cost_estimate=pl.CostEstimate(flops=0, bytes_accessed=4 * b * n * count, transcendentals=0),
        name="halves",
    )(minus, plus, *others)


def relay(v, shift, others=()):
    minus, plus = shift(v, 1), shift(v, -1)
    first, second = halves(minus, plus, others)
    return [v, minus, plus, shift(first, 1), shift(second, -1)]


def join(pieces):
    _, b, n = pieces[0].shape
    step = 512

    def kernel(*refs):
        at = 0
        for ref in refs[:-1]:
            refs[-1][at : at + ref.shape[0]] = ref[...]
            at += ref.shape[0]

    total = sum(p.shape[0] for p in pieces)
    return pl.pallas_call(
        kernel,
        grid=(n // step,),
        in_specs=[pl.BlockSpec((p.shape[0], b, step), lambda i: (0, 0, i)) for p in pieces],
        out_specs=pl.BlockSpec((total, b, step), lambda i: (0, 0, i)),
        out_shape=jax.ShapeDtypeStruct((total, b, n), jnp.bfloat16),
        compiler_params=PARAMS,
        cost_estimate=pl.CostEstimate(flops=0, bytes_accessed=4 * b * n * total, transcendentals=0),
        name="join",
    )(*pieces)


ROW, OTHER, X, CORE, Z, Y, COL = range(7)


def place_of(distance):
    return jnp.where(distance == 0, 0, jnp.where(distance == 3, 1, jnp.where(distance == 1, 2, 3)))


def choose_kernel(at_ref, size_ref, density_ref, own_ref, other_ref, pattern_ref, out_ref):
    t = pl.program_id(0)
    x, core = at_ref[X], at_ref[CORE]
    pair = 2 * lax.rem(x + t // 2, 4) + lax.rem(core + lax.rem(t, 2), 2)
    i32 = jnp.int32
    sub = lax.broadcasted_iota(i32, (8, BESIDE), 0)
    lane = lax.broadcasted_iota(i32, (1, BESIDE), 1)
    unit = lax.rem(lane, 64)
    spot = jnp.zeros_like(sub)
    for i, d in enumerate(ORDER):
        spot = jnp.where(sub // 2 == i, 2 * lax.rem(x + (d + 4), 4), spot)
    spot = spot + lax.rem(sub, 2)
    rows, patterns = [], []
    for b in range(2):
        away_y = lax.rem(2 * core + b - at_ref[Y] + 4, 4)
        away_z = lax.rem(x - at_ref[Z] + 4, 4)
        piece = 4 * place_of(away_y) + place_of(away_z)
        own, other = own_ref[piece].astype(i32), other_ref[piece].astype(i32)
        atoms = []
        for names in (jnp.where(core == 0, own, other), jnp.where(core == 0, other, own)):
            match = names // 8 == pair
            low = jnp.min(jnp.where(match, spot, 99), axis=0, keepdims=True)
            high = jnp.max(jnp.where(match, spot, -1), axis=0, keepdims=True)
            atom = names - 8 * pair
            one = jnp.max(jnp.where(match & (spot == low), atom, -1), axis=0, keepdims=True)
            two = jnp.max(jnp.where(match & (spot == high) & (high > low), atom, -1), axis=0, keepdims=True)
            atoms.append((one, two))
        slots = [jnp.where(atoms[j][0] >= 0, atoms[j][0], atoms[1 - j][1]) for j in range(2)]
        atom = jnp.where(lane < 64, slots[0], slots[1])
        size = jnp.zeros_like(atom)
        pattern = jnp.zeros((8, BESIDE), jnp.float32)
        for j in range(8):
            size = jnp.where(atom == j, size_ref[16 * at_ref[ROW] + 8 * b + j], size)
            pattern = jnp.where(atom == j, pattern_ref[:, 8 * b + j : 8 * b + j + 1].astype(jnp.float32), pattern)
        rows.append(jnp.where((atom >= 0) & (unit < size), (8 * b + atom) * 64 + unit, -1))
        patterns.append(pattern)
    rows, pattern = jnp.concatenate(rows, axis=1), jnp.concatenate(patterns, axis=1)
    hit = lax.broadcasted_iota(i32, (density_ref.shape[1], rows.shape[1]), 0) == rows
    picked = jnp.dot(density_ref[...], hit.astype(jnp.bfloat16), preferred_element_type=jnp.float32)
    row = lax.broadcasted_iota(i32, (64, rows.shape[1]), 0)
    for j in range(8):
        factor = jnp.where(row < size_ref[8 * at_ref[COL] + j], pattern[j : j + 1], 0.0)
        out_ref[0, 64 * j : 64 * j + 64] = (picked[64 * j : 64 * j + 64] * factor).astype(jnp.bfloat16)


def choose_columns(at, sizes, density, own, other, pattern):
    m, width = density.shape
    names = pl.BlockSpec(own.shape, lambda t, p, q: (0, 0, 0))
    return pl.pallas_call(
        choose_kernel,
        grid_spec=pltpu.PrefetchScalarGridSpec(
            num_scalar_prefetch=2,
            grid=(8,),
            in_specs=[
                pl.BlockSpec((m, width), lambda t, p, q: (0, 0)),
                names,
                names,
                pl.BlockSpec(pattern.shape, lambda t, p, q: (0, 0)),
            ],
            out_specs=pl.BlockSpec((1, m, 256), lambda t, p, q: (t, 0, 0)),
        ),
        out_shape=jax.ShapeDtypeStruct((8, m, 256), jnp.bfloat16),
        compiler_params=PARAMS,
        cost_estimate=pl.CostEstimate(flops=2 * m * width * 2048, bytes_accessed=2 * m * (width + 2048), transcendentals=0),
        name="choose_columns",
    )(at, sizes, density, own, other, pattern)


def order_kernel(at_ref, *refs):
    own, other, (left1, left2), (blocks, sems) = refs[:4], refs[4], refs[5:7], refs[7:]
    copies = [pltpu.make_async_copy(own[d].at[0], blocks.at[d], sems.at[d]) for d in range(4)]
    copies += [pltpu.make_async_copy(other.at[d], blocks.at[4 + d], sems.at[4 + d]) for d in range(4)]
    for copy in copies:
        copy.start()
    for copy in copies:
        copy.wait()
    for i in range(16):
        j = (i % 4) * 4 + i // 4
        from_y = lax.rem(at_ref[Y] + (ORDER[i // 4] + 4), 4)
        from_z = lax.rem(at_ref[Z] + (ORDER[i % 4] + 4), 4)
        place = lax.rem(at_ref[X] - from_z + 4, 4) + jnp.where(from_y // 2 == at_ref[CORE], 0, 4)
        block = blocks[place, :, pl.ds(pl.multiple_of(lax.rem(from_y, 2) * 128, 128), 128)]
        left1[:, i * 128 : (i + 1) * 128] = block
        left2[:, j * 128 : (j + 1) * 128] = block


def order_columns(at, own, other):
    m = other.shape[1]
    return pl.pallas_call(
        order_kernel,
        grid_spec=pltpu.PrefetchScalarGridSpec(
            num_scalar_prefetch=1,
            grid=(1,),
            in_specs=[ANY] * 5,
            out_specs=[pl.BlockSpec((m, 2048), lambda i, p: (0, 0))] * 2,
            scratch_shapes=[pltpu.VMEM((8, m, 256), jnp.bfloat16), pltpu.SemaphoreType.DMA((8,))],
        ),
        out_shape=[jax.ShapeDtypeStruct((m, 2048), jnp.bfloat16)] * 2,
        compiler_params=PARAMS,
        cost_estimate=pl.CostEstimate(flops=0, bytes_accessed=8 * 2 * m * 2048, transcendentals=0),
        name="order_columns",
    )(at, *own, other)


def pick_tiles(at, names, pieces, which):
    _, b, n = pieces[0].shape
    step = 1024

    def kernel(at_ref, name_ref, *refs):
        pieces, out = refs[:5], refs[5]
        spots = [2 * lax.rem(at_ref[X] + (d + 4), 4) + s for d in ORDER for s in range(2)]
        match = [(name_ref[j] // 8 == at_ref[which]).astype(jnp.int32) for j in range(8)]
        slots = []
        for j in range(8):
            before = sum(match[i] * (spots[i] < spots[j]).astype(jnp.int32) for i in range(8) if i != j)
            slots.append(jnp.where(at_ref[CORE] == 1, 1 - before, before))
        for s in range(2):
            there = [match[j] * (slots[j] == s).astype(jnp.int32) for j in range(8)]

            @pl.when(sum(there) == 0)
            def _():
                out[s] = jnp.zeros(out.shape[1:], out.dtype)

            for j in range(8):

                @pl.when(there[j] == 1)
                def _():
                    out[s] = pieces[j // 2][j % 2] if j < 6 else pieces[j - 3][0]

    return pl.pallas_call(
        kernel,
        grid_spec=pltpu.PrefetchScalarGridSpec(
            num_scalar_prefetch=2,
            grid=(n // step,),
            in_specs=[pl.BlockSpec((v.shape[0], b, step), lambda i, p, q: (0, 0, i)) for v in pieces],
            out_specs=pl.BlockSpec((2, b, step), lambda i, p, q: (0, 0, i)),
        ),
        out_shape=jax.ShapeDtypeStruct((2, b, n), jnp.bfloat16),
        compiler_params=PARAMS,
        cost_estimate=pl.CostEstimate(flops=0, bytes_accessed=24 * b * n, transcendentals=0),
        name="pick_tiles",
    )(at, names, *pieces)


def merge_tiles(mine, got, cuts):
    _, b, n = mine.shape
    edges = [0, *cuts, n]

    def kernel(mine_ref, got_ref, *outs):
        for out, low, high in zip(outs, edges, edges[1:]):
            out[...] = mine_ref[:, :, low:high] + got_ref[:, :, low:high]

    return pl.pallas_call(
        kernel,
        out_shape=[jax.ShapeDtypeStruct((2, b, v - u), jnp.bfloat16) for u, v in zip(edges, edges[1:])],
        compiler_params=PARAMS,
        cost_estimate=pl.CostEstimate(flops=0, bytes_accessed=12 * b * n, transcendentals=0),
        name="merge_tiles",
    )(mine, got)


def product_kernel(at, count, started, left_ref, *refs):
    total = refs[count][...] if started else None
    for piece in refs[:count]:
        depth = piece.shape[0] * piece.shape[1]
        right = piece[...].reshape(depth, piece.shape[2])
        term = jnp.dot(left_ref[:, at : at + depth], right, preferred_element_type=jnp.float32)
        total = term if total is None else total + term
        at += depth
    refs[-1][...] = total.astype(refs[-1].dtype)


def product(left, at, pieces, n, total=None, out=None, column=0, width=None):
    m = left.shape[0]
    step = 512
    depth = sum(p.shape[0] * p.shape[1] for p in pieces)
    first = column // step
    specs = [pl.BlockSpec(left.shape, lambda i: (0, 0))]
    specs += [pl.BlockSpec(p.shape[:2] + (step,), lambda i: (0, 0, i)) for p in pieces]
    operands = [left, *pieces]
    if total is not None:
        specs.append(pl.BlockSpec((m, step), lambda i: (0, i)))
        operands.append(total)
    alias = {}
    if out is not None:
        specs.append(pl.BlockSpec(memory_space=pl.ANY))
        alias = {len(operands): 0}
        operands.append(out)

    def kernel(*refs):
        product_kernel(at, len(pieces), total is not None, *refs)

    shape = jax.ShapeDtypeStruct((m, n), jnp.float32) if width is None else jax.ShapeDtypeStruct((m, width), jnp.bfloat16)
    return pl.pallas_call(
        kernel,
        grid=(n // step,),
        in_specs=specs,
        out_specs=pl.BlockSpec((m, step), lambda i: (0, first + i)),
        out_shape=shape,
        input_output_aliases=alias,
        compiler_params=PARAMS,
        cost_estimate=pl.CostEstimate(
            flops=2 * WEIGHT * m * depth * n, bytes_accessed=2 * WEIGHT * (left.size + (depth + 2 * m) * n), transcendentals=0
        ),
        name="product",
    )(*operands)


def per_device(blocks, block_atom, block_pair, atom_sizes, density, density_pattern):
    b, width = blocks.shape[1], blocks.shape[2]
    r, c = lax.axis_index("row"), lax.axis_index("col")
    x, k, z, y = r // 2, r % 2, c // 4, c % 4
    i32 = jnp.int32
    at = jnp.stack([r, r + 1 - 2 * k, x, k, z, y, c]).astype(i32)

    def around(v, shift):
        return [v, shift(v, 1), shift(v, -1), shift(v, 2)]

    def forward(sides, shift):
        first, second = halves(*sides)
        return [shift(first, 1), shift(second, -1)]

    name = (8 * block_pair + jnp.clip(block_atom - 8 * c, 0, 7)).astype(jnp.float32)
    name = jnp.stack(around(jnp.broadcast_to(name, (2, BESIDE)), shift_z))
    near = relay(blocks, shift_row_x, (name,))
    name = jnp.concatenate(around(name, shift_y))
    names = jnp.concatenate(around(name, shift_row_x), axis=1)

    here = names[0, :, 0].astype(i32)
    theirs = swap_core(pick_tiles(at, here, near, OTHER))
    v1, v2 = merge_tiles(pick_tiles(at, here, near, ROW), theirs, [width // 2])
    pieces1, pieces2 = relay(v1, shift_z), relay(v2, shift_y)

    chosen = choose_columns(at, atom_sizes, density, names, swap_core(names), density_pattern)
    chosen = chosen.reshape(4, 2, 8 * b, 4 * b)
    own = [chosen[0]] + [shift_row_x(chosen[d], d) for d in (1, 2, 3)]

    g1, g2 = join(pieces1), join(pieces2)
    sides1, sides2 = [shift_y(g1, 1), shift_y(g1, -1)], [shift_z(g2, 1), shift_z(g2, -1)]
    last1, last2 = forward(sides1, shift_y), forward(sides2, shift_z)

    other = swap_core(jnp.stack([piece[1] for piece in own]))
    left1, left2 = order_columns(at, own, other)

    half = width // 2
    total1 = product(left1, 0, [g1, *sides1], half)
    total2 = product(left2, 0, [g2, *sides2], half)
    out = product(left1, 24 * b, last1, half, total1, None, 0, width)
    out = product(left2, 24 * b, last2, half, total2, out, half, width)
    return out[None]


def solution(mesh):
    placed = (
        P("row", "col", None),
        P("row", "col"),
        P("row", "col"),
        P(),
        P("col", "row"),
        P("col", "row"),
    )
    return jax.shard_map(
        per_device, mesh=mesh, in_specs=placed, out_specs=P("row", "col", None), check_vma=False
    )
```

```python
import jax
import jax.numpy as jnp
from jax import lax
from jax.experimental import pallas as pl
from jax.experimental.pallas import tpu as pltpu
from jax.sharding import PartitionSpec as P

ORDER = (0, -1, 1, 2)
VMEM = 14 * 1024 * 1024
BESIDE = 128
WEIGHT = 2
PARAMS = pltpu.CompilerParams(vmem_limit_bytes=VMEM)
ANY = pl.BlockSpec(memory_space=pl.ANY)


def shift_row_x(v, d):
    return lax.ppermute(v, "row", [(2 * x + k, 2 * ((x + d) % 4) + k) for x in range(4) for k in range(2)])


def swap_core(v):
    return lax.ppermute(v, "row", [(r, r ^ 1) for r in range(8)])


def shift_z(v, d):
    return lax.ppermute(v, "col", [(4 * z + y, 4 * ((z + d) % 4) + y) for z in range(4) for y in range(4)])


def shift_y(v, d):
    return lax.ppermute(v, "col", [(4 * z + y, 4 * z + (y + d) % 4) for z in range(4) for y in range(4)])


def halves(minus, plus, others=()):
    count, b, n = minus.shape
    half, step = count // 2, min(n, 1024)

    def kernel(*refs):
        refs[-2][...] = refs[0][...]
        refs[-1][...] = refs[1][...]

    spec = pl.BlockSpec((half, b, step), lambda i: (0, 0, i))
    return pl.pallas_call(
        kernel,
        grid=(n // step,),
        in_specs=[spec, pl.BlockSpec((half, b, step), lambda i: (1, 0, i))] + [ANY] * len(others),
        out_specs=[spec, spec],
        out_shape=[jax.ShapeDtypeStruct((half, b, n), jnp.bfloat16)] * 2,
        compiler_params=PARAMS,
        cost_estimate=pl.CostEstimate(flops=0, bytes_accessed=4 * b * n * count, transcendentals=0),
        name="halves",
    )(minus, plus, *others)


def relay(v, shift, others=()):
    minus, plus = shift(v, 1), shift(v, -1)
    first, second = halves(minus, plus, others)
    return [v, minus, plus, shift(first, 1), shift(second, -1)]


def join(pieces):
    _, b, n = pieces[0].shape
    step = 512

    def kernel(*refs):
        at = 0
        for ref in refs[:-1]:
            refs[-1][at : at + ref.shape[0]] = ref[...]
            at += ref.shape[0]

    total = sum(p.shape[0] for p in pieces)
    return pl.pallas_call(
        kernel,
        grid=(n // step,),
        in_specs=[pl.BlockSpec((p.shape[0], b, step), lambda i: (0, 0, i)) for p in pieces],
        out_specs=pl.BlockSpec((total, b, step), lambda i: (0, 0, i)),
        out_shape=jax.ShapeDtypeStruct((total, b, n), jnp.bfloat16),
        compiler_params=PARAMS,
        cost_estimate=pl.CostEstimate(flops=0, bytes_accessed=4 * b * n * total, transcendentals=0),
        name="join",
    )(*pieces)


ROW, OTHER, X, CORE, Z, Y, COL = range(7)


def place_of(distance):
    return jnp.where(distance == 0, 0, jnp.where(distance == 3, 1, jnp.where(distance == 1, 2, 3)))


def choose_kernel(at_ref, size_ref, density_ref, own_ref, other_ref, pattern_ref, out_ref):
    t = pl.program_id(0)
    x, core = at_ref[X], at_ref[CORE]
    pair = 2 * lax.rem(x + t // 2, 4) + lax.rem(core + lax.rem(t, 2), 2)
    i32 = jnp.int32
    sub = lax.broadcasted_iota(i32, (8, BESIDE), 0)
    lane = lax.broadcasted_iota(i32, (1, BESIDE), 1)
    unit = lax.rem(lane, 64)
    spot = jnp.zeros_like(sub)
    for i, d in enumerate(ORDER):
        spot = jnp.where(sub // 2 == i, 2 * lax.rem(x + (d + 4), 4), spot)
    spot = spot + lax.rem(sub, 2)
    rows, patterns = [], []
    for b in range(2):
        away_y = lax.rem(2 * core + b - at_ref[Y] + 4, 4)
        away_z = lax.rem(x - at_ref[Z] + 4, 4)
        piece = 4 * place_of(away_y) + place_of(away_z)
        own, other = own_ref[piece].astype(i32), other_ref[piece].astype(i32)
        atoms = []
        for names in (jnp.where(core == 0, own, other), jnp.where(core == 0, other, own)):
            match = names // 8 == pair
            low = jnp.min(jnp.where(match, spot, 99), axis=0, keepdims=True)
            high = jnp.max(jnp.where(match, spot, -1), axis=0, keepdims=True)
            atom = names - 8 * pair
            one = jnp.max(jnp.where(match & (spot == low), atom, -1), axis=0, keepdims=True)
            two = jnp.max(jnp.where(match & (spot == high) & (high > low), atom, -1), axis=0, keepdims=True)
            atoms.append((one, two))
        slots = [jnp.where(atoms[j][0] >= 0, atoms[j][0], atoms[1 - j][1]) for j in range(2)]
        atom = jnp.where(lane < 64, slots[0], slots[1])
        size = jnp.zeros_like(atom)
        pattern = jnp.zeros((8, BESIDE), jnp.float32)
        for j in range(8):
            size = jnp.where(atom == j, size_ref[16 * at_ref[ROW] + 8 * b + j], size)
            pattern = jnp.where(atom == j, pattern_ref[:, 8 * b + j : 8 * b + j + 1].astype(jnp.float32), pattern)
        rows.append(jnp.where((atom >= 0) & (unit < size), (8 * b + atom) * 64 + unit, -1))
        patterns.append(pattern)
    rows, pattern = jnp.concatenate(rows, axis=1), jnp.concatenate(patterns, axis=1)
    hit = lax.broadcasted_iota(i32, (density_ref.shape[1], rows.shape[1]), 0) == rows
    picked = jnp.dot(density_ref[...], hit.astype(jnp.bfloat16), preferred_element_type=jnp.float32)
    row = lax.broadcasted_iota(i32, (64, rows.shape[1]), 0)
    for j in range(8):
        factor = jnp.where(row < size_ref[8 * at_ref[COL] + j], pattern[j : j + 1], 0.0)
        out_ref[0, 64 * j : 64 * j + 64] = (picked[64 * j : 64 * j + 64] * factor).astype(jnp.bfloat16)


def choose_columns(at, sizes, density, own, other, pattern):
    m, width = density.shape
    names = pl.BlockSpec(own.shape, lambda t, p, q: (0, 0, 0))
    return pl.pallas_call(
        choose_kernel,
        grid_spec=pltpu.PrefetchScalarGridSpec(
            num_scalar_prefetch=2,
            grid=(8,),
            in_specs=[
                pl.BlockSpec((m, width), lambda t, p, q: (0, 0)),
                names,
                names,
                pl.BlockSpec(pattern.shape, lambda t, p, q: (0, 0)),
            ],
            out_specs=pl.BlockSpec((1, m, 256), lambda t, p, q: (t, 0, 0)),
        ),
        out_shape=jax.ShapeDtypeStruct((8, m, 256), jnp.bfloat16),
        compiler_params=PARAMS,
        cost_estimate=pl.CostEstimate(flops=2 * m * width * 2048, bytes_accessed=2 * m * (width + 2048), transcendentals=0),
        name="choose_columns",
    )(at, sizes, density, own, other, pattern)


def order_kernel(at_ref, *refs):
    own, other, (left1, left2), (blocks, sems) = refs[:4], refs[4], refs[5:7], refs[7:]
    copies = [pltpu.make_async_copy(own[d].at[0], blocks.at[d], sems.at[d]) for d in range(4)]
    copies += [pltpu.make_async_copy(other.at[d], blocks.at[4 + d], sems.at[4 + d]) for d in range(4)]
    for copy in copies:
        copy.start()
    for copy in copies:
        copy.wait()
    for i in range(16):
        j = (i % 4) * 4 + i // 4
        from_y = lax.rem(at_ref[Y] + (ORDER[i // 4] + 4), 4)
        from_z = lax.rem(at_ref[Z] + (ORDER[i % 4] + 4), 4)
        place = lax.rem(at_ref[X] - from_z + 4, 4) + jnp.where(from_y // 2 == at_ref[CORE], 0, 4)
        block = blocks[place, :, pl.ds(pl.multiple_of(lax.rem(from_y, 2) * 128, 128), 128)]
        left1[:, i * 128 : (i + 1) * 128] = block
        left2[:, j * 128 : (j + 1) * 128] = block


def order_columns(at, own, other):
    m = other.shape[1]
    return pl.pallas_call(
        order_kernel,
        grid_spec=pltpu.PrefetchScalarGridSpec(
            num_scalar_prefetch=1,
            grid=(1,),
            in_specs=[ANY] * 5,
            out_specs=[pl.BlockSpec((m, 2048), lambda i, p: (0, 0))] * 2,
            scratch_shapes=[pltpu.VMEM((8, m, 256), jnp.bfloat16), pltpu.SemaphoreType.DMA((8,))],
        ),
        out_shape=[jax.ShapeDtypeStruct((m, 2048), jnp.bfloat16)] * 2,
        compiler_params=PARAMS,
        cost_estimate=pl.CostEstimate(flops=0, bytes_accessed=8 * 2 * m * 2048, transcendentals=0),
        name="order_columns",
    )(at, *own, other)


def pick_tiles(at, names, pieces, which):
    _, b, n = pieces[0].shape

    def kernel(at_ref, name_ref, *refs):
        pieces, (out, zeros, sems) = refs[:5], refs[5:]
        spots = [2 * lax.rem(at_ref[X] + (d + 4), 4) + s for d in ORDER for s in range(2)]
        match = [(name_ref[j] // 8 == at_ref[which]).astype(jnp.int32) for j in range(8)]
        slots = []
        for j in range(8):
            before = sum(match[i] * (spots[i] < spots[j]).astype(jnp.int32) for i in range(8) if i != j)
            slots.append(jnp.where(at_ref[CORE] == 1, 1 - before, before))
        for s in range(2):
            there = [match[j] * (slots[j] == s).astype(jnp.int32) for j in range(8)]

            @pl.when(sum(there) == 0)
            def _():
                zeros[...] = jnp.zeros_like(zeros)
                pltpu.make_async_copy(zeros, out.at[s], sems.at[s]).start()

            for j in range(8):

                @pl.when(there[j] == 1)
                def _():
                    source = pieces[j // 2].at[j % 2] if j < 6 else pieces[j - 3].at[0]
                    pltpu.make_async_copy(source, out.at[s], sems.at[s]).start()

        for s in range(2):
            pltpu.make_async_copy(zeros, out.at[s], sems.at[s]).wait()

    return pl.pallas_call(
        kernel,
        grid_spec=pltpu.PrefetchScalarGridSpec(
            num_scalar_prefetch=2,
            grid=(1,),
            in_specs=[ANY] * 5,
            out_specs=ANY,
            scratch_shapes=[pltpu.VMEM((b, n), jnp.bfloat16), pltpu.SemaphoreType.DMA((2,))],
        ),
        out_shape=jax.ShapeDtypeStruct((2, b, n), jnp.bfloat16),
        compiler_params=PARAMS,
        cost_estimate=pl.CostEstimate(flops=0, bytes_accessed=8 * b * n, transcendentals=0),
        name="pick_tiles",
    )(at, names, *pieces)


def merge_tiles(mine, got, cuts):
    _, b, n = mine.shape
    edges = [0, *cuts, n]

    def kernel(mine_ref, got_ref, *outs):
        for out, low, high in zip(outs, edges, edges[1:]):
            out[...] = mine_ref[:, :, low:high] + got_ref[:, :, low:high]

    return pl.pallas_call(
        kernel,
        out_shape=[jax.ShapeDtypeStruct((2, b, v - u), jnp.bfloat16) for u, v in zip(edges, edges[1:])],
        compiler_params=PARAMS,
        cost_estimate=pl.CostEstimate(flops=0, bytes_accessed=12 * b * n, transcendentals=0),
        name="merge_tiles",
    )(mine, got)


def product_kernel(at, count, started, left_ref, *refs):
    total = refs[count][...] if started else None
    for piece in refs[:count]:
        depth = piece.shape[0] * piece.shape[1]
        right = piece[...].reshape(depth, piece.shape[2])
        term = jnp.dot(left_ref[:, at : at + depth], right, preferred_element_type=jnp.float32)
        total = term if total is None else total + term
        at += depth
    refs[-1][...] = total.astype(refs[-1].dtype)


def product(left, at, pieces, n, total=None, out=None, column=0, width=None):
    m = left.shape[0]
    step = 512
    depth = sum(p.shape[0] * p.shape[1] for p in pieces)
    first = column // step
    specs = [pl.BlockSpec(left.shape, lambda i: (0, 0))]
    specs += [pl.BlockSpec(p.shape[:2] + (step,), lambda i: (0, 0, i)) for p in pieces]
    operands = [left, *pieces]
    if total is not None:
        specs.append(pl.BlockSpec((m, step), lambda i: (0, i)))
        operands.append(total)
    alias = {}
    if out is not None:
        specs.append(pl.BlockSpec(memory_space=pl.ANY))
        alias = {len(operands): 0}
        operands.append(out)

    def kernel(*refs):
        product_kernel(at, len(pieces), total is not None, *refs)

    shape = jax.ShapeDtypeStruct((m, n), jnp.float32) if width is None else jax.ShapeDtypeStruct((m, width), jnp.bfloat16)
    return pl.pallas_call(
        kernel,
        grid=(n // step,),
        in_specs=specs,
        out_specs=pl.BlockSpec((m, step), lambda i: (0, first + i)),
        out_shape=shape,
        input_output_aliases=alias,
        compiler_params=PARAMS,
        cost_estimate=pl.CostEstimate(
            flops=2 * WEIGHT * m * depth * n, bytes_accessed=2 * WEIGHT * (left.size + (depth + 2 * m) * n), transcendentals=0
        ),
        name="product",
    )(*operands)


def per_device(blocks, block_atom, block_pair, atom_sizes, density, density_pattern):
    b, width = blocks.shape[1], blocks.shape[2]
    r, c = lax.axis_index("row"), lax.axis_index("col")
    x, k, z, y = r // 2, r % 2, c // 4, c % 4
    i32 = jnp.int32
    at = jnp.stack([r, r + 1 - 2 * k, x, k, z, y, c]).astype(i32)

    def around(v, shift):
        return [v, shift(v, 1), shift(v, -1), shift(v, 2)]

    def forward(sides, shift):
        first, second = halves(*sides)
        return [shift(first, 1), shift(second, -1)]

    name = (8 * block_pair + jnp.clip(block_atom - 8 * c, 0, 7)).astype(jnp.float32)
    name = jnp.stack(around(jnp.broadcast_to(name, (2, BESIDE)), shift_z))
    near = relay(blocks, shift_row_x, (name,))
    name = jnp.concatenate(around(name, shift_y))
    names = jnp.concatenate(around(name, shift_row_x), axis=1)

    here = names[0, :, 0].astype(i32)
    theirs = swap_core(pick_tiles(at, here, near, OTHER))
    v1, v2 = merge_tiles(pick_tiles(at, here, near, ROW), theirs, [width // 2])
    pieces1, pieces2 = relay(v1, shift_z), relay(v2, shift_y)

    chosen = choose_columns(at, atom_sizes, density, names, swap_core(names), density_pattern)
    chosen = chosen.reshape(4, 2, 8 * b, 4 * b)
    own = [chosen[0]] + [shift_row_x(chosen[d], d) for d in (1, 2, 3)]

    g1, g2 = join(pieces1), join(pieces2)
    sides1, sides2 = [shift_y(g1, 1), shift_y(g1, -1)], [shift_z(g2, 1), shift_z(g2, -1)]
    last1, last2 = forward(sides1, shift_y), forward(sides2, shift_z)

    other = swap_core(jnp.stack([piece[1] for piece in own]))
    left1, left2 = order_columns(at, own, other)

    half = width // 2
    total1 = product(left1, 0, [g1, *sides1], half)
    total2 = product(left2, 0, [g2, *sides2], half)
    out = product(left1, 24 * b, last1, half, total1, None, 0, width)
    out = product(left2, 24 * b, last2, half, total2, out, half, width)
    return out[None]


def solution(mesh):
    placed = (
        P("row", "col", None),
        P("row", "col"),
        P("row", "col"),
        P(),
        P("col", "row"),
        P("col", "row"),
    )
    return jax.shard_map(
        per_device, mesh=mesh, in_specs=placed, out_specs=P("row", "col", None), check_vma=False
    )
```

```python
import functools

import jax
import jax.numpy as jnp
from jax import lax
from jax.experimental import pallas as pl
from jax.experimental.pallas import tpu as pltpu
from jax.sharding import PartitionSpec as P

ORDER = (0, -1, 1, 2)
VMEM = 14 * 1024 * 1024
BESIDE = 128
WEIGHT = 2
PARAMS = pltpu.CompilerParams(vmem_limit_bytes=VMEM)
ANY = pl.BlockSpec(memory_space=pl.ANY)


def shift_row_x(v, d):
    return lax.ppermute(v, "row", [(2 * x + k, 2 * ((x + d) % 4) + k) for x in range(4) for k in range(2)])


def swap_core(v):
    return lax.ppermute(v, "row", [(r, r ^ 1) for r in range(8)])


def shift_z(v, d):
    return lax.ppermute(v, "col", [(4 * z + y, 4 * ((z + d) % 4) + y) for z in range(4) for y in range(4)])


def shift_y(v, d):
    return lax.ppermute(v, "col", [(4 * z + y, 4 * z + (y + d) % 4) for z in range(4) for y in range(4)])


def halves(minus, plus, others=()):
    count, b, n = minus.shape
    half, step = count // 2, min(n, 1024)

    def kernel(*refs):
        refs[-2][...] = refs[0][...]
        refs[-1][...] = refs[1][...]

    spec = pl.BlockSpec((half, b, step), lambda i: (0, 0, i))
    return pl.pallas_call(
        kernel,
        grid=(n // step,),
        in_specs=[spec, pl.BlockSpec((half, b, step), lambda i: (1, 0, i))] + [ANY] * len(others),
        out_specs=[spec, spec],
        out_shape=[jax.ShapeDtypeStruct((half, b, n), jnp.bfloat16)] * 2,
        compiler_params=PARAMS,
        cost_estimate=pl.CostEstimate(flops=0, bytes_accessed=4 * b * n * count, transcendentals=0),
        name="halves",
    )(minus, plus, *others)


def relay(v, shift, others=()):
    minus, plus = shift(v, 1), shift(v, -1)
    first, second = halves(minus, plus, others)
    return [v, minus, plus, shift(first, 1), shift(second, -1)]


def join(pieces):
    _, b, n = pieces[0].shape
    step = 512

    def kernel(*refs):
        at = 0
        for ref in refs[:-1]:
            refs[-1][at : at + ref.shape[0]] = ref[...]
            at += ref.shape[0]

    total = sum(p.shape[0] for p in pieces)
    return pl.pallas_call(
        kernel,
        grid=(n // step,),
        in_specs=[pl.BlockSpec((p.shape[0], b, step), lambda i: (0, 0, i)) for p in pieces],
        out_specs=pl.BlockSpec((total, b, step), lambda i: (0, 0, i)),
        out_shape=jax.ShapeDtypeStruct((total, b, n), jnp.bfloat16),
        compiler_params=PARAMS,
        cost_estimate=pl.CostEstimate(flops=0, bytes_accessed=4 * b * n * total, transcendentals=0),
        name="join",
    )(*pieces)


ROW, OTHER, X, CORE, Z, Y, COL = range(7)


def place_of(distance):
    return jnp.where(distance == 0, 0, jnp.where(distance == 3, 1, jnp.where(distance == 1, 2, 3)))


def choose_kernel(d, at_ref, size_ref, density_ref, own_ref, other_ref, pattern_ref, out_ref):
    x, core = at_ref[X], at_ref[CORE]
    pair = 2 * lax.rem(x + d, 4) + lax.rem(core + pl.program_id(0), 2)
    i32 = jnp.int32
    sub = lax.broadcasted_iota(i32, (8, BESIDE), 0)
    lane = lax.broadcasted_iota(i32, (1, BESIDE), 1)
    unit = lax.rem(lane, 64)
    spot = jnp.zeros_like(sub)
    for i, d in enumerate(ORDER):
        spot = jnp.where(sub // 2 == i, 2 * lax.rem(x + (d + 4), 4), spot)
    spot = spot + lax.rem(sub, 2)
    rows, patterns = [], []
    for b in range(2):
        away_y = lax.rem(2 * core + b - at_ref[Y] + 4, 4)
        away_z = lax.rem(x - at_ref[Z] + 4, 4)
        piece = 4 * place_of(away_y) + place_of(away_z)
        own, other = own_ref[piece].astype(i32), other_ref[piece].astype(i32)
        atoms = []
        for names in (jnp.where(core == 0, own, other), jnp.where(core == 0, other, own)):
            match = names // 8 == pair
            low = jnp.min(jnp.where(match, spot, 99), axis=0, keepdims=True)
            high = jnp.max(jnp.where(match, spot, -1), axis=0, keepdims=True)
            atom = names - 8 * pair
            one = jnp.max(jnp.where(match & (spot == low), atom, -1), axis=0, keepdims=True)
            two = jnp.max(jnp.where(match & (spot == high) & (high > low), atom, -1), axis=0, keepdims=True)
            atoms.append((one, two))
        slots = [jnp.where(atoms[j][0] >= 0, atoms[j][0], atoms[1 - j][1]) for j in range(2)]
        atom = jnp.where(lane < 64, slots[0], slots[1])
        size = jnp.zeros_like(atom)
        pattern = jnp.zeros((8, BESIDE), jnp.float32)
        for j in range(8):
            size = jnp.where(atom == j, size_ref[16 * at_ref[ROW] + 8 * b + j], size)
            pattern = jnp.where(atom == j, pattern_ref[:, 8 * b + j : 8 * b + j + 1].astype(jnp.float32), pattern)
        rows.append(jnp.where((atom >= 0) & (unit < size), (8 * b + atom) * 64 + unit, -1))
        patterns.append(pattern)
    rows, pattern = jnp.concatenate(rows, axis=1), jnp.concatenate(patterns, axis=1)
    hit = lax.broadcasted_iota(i32, (density_ref.shape[1], rows.shape[1]), 0) == rows
    picked = jnp.dot(density_ref[...], hit.astype(jnp.bfloat16), preferred_element_type=jnp.float32)
    row = lax.broadcasted_iota(i32, (64, rows.shape[1]), 0)
    for j in range(8):
        factor = jnp.where(row < size_ref[8 * at_ref[COL] + j], pattern[j : j + 1], 0.0)
        out_ref[0, 64 * j : 64 * j + 64] = (picked[64 * j : 64 * j + 64] * factor).astype(jnp.bfloat16)


def choose_columns(at, sizes, density, own, other, pattern, d):
    m, width = density.shape
    names = pl.BlockSpec(own.shape, lambda t, p, q: (0, 0, 0))
    return pl.pallas_call(
        functools.partial(choose_kernel, d),
        grid_spec=pltpu.PrefetchScalarGridSpec(
            num_scalar_prefetch=2,
            grid=(2,),
            in_specs=[
                pl.BlockSpec((m, width), lambda t, p, q: (0, 0)),
                names,
                names,
                pl.BlockSpec(pattern.shape, lambda t, p, q: (0, 0)),
            ],
            out_specs=pl.BlockSpec((1, m, 256), lambda t, p, q: (t, 0, 0)),
        ),
        out_shape=jax.ShapeDtypeStruct((2, m, 256), jnp.bfloat16),
        compiler_params=PARAMS,
        cost_estimate=pl.CostEstimate(flops=2 * m * width * 512, bytes_accessed=2 * m * (width + 512), transcendentals=0),
        name="choose_columns",
    )(at, sizes, density, own, other, pattern)


def order_kernel(at_ref, *refs):
    own, other, (left1, left2), (blocks, sems) = refs[:4], refs[4], refs[5:7], refs[7:]
    copies = [pltpu.make_async_copy(own[d].at[0], blocks.at[d], sems.at[d]) for d in range(4)]
    copies += [pltpu.make_async_copy(other.at[d], blocks.at[4 + d], sems.at[4 + d]) for d in range(4)]
    for copy in copies:
        copy.start()
    for copy in copies:
        copy.wait()
    for i in range(16):
        j = (i % 4) * 4 + i // 4
        from_y = lax.rem(at_ref[Y] + (ORDER[i // 4] + 4), 4)
        from_z = lax.rem(at_ref[Z] + (ORDER[i % 4] + 4), 4)
        place = lax.rem(at_ref[X] - from_z + 4, 4) + jnp.where(from_y // 2 == at_ref[CORE], 0, 4)
        block = blocks[place, :, pl.ds(pl.multiple_of(lax.rem(from_y, 2) * 128, 128), 128)]
        left1[:, i * 128 : (i + 1) * 128] = block
        left2[:, j * 128 : (j + 1) * 128] = block


def order_columns(at, own, other):
    m = other.shape[1]
    return pl.pallas_call(
        order_kernel,
        grid_spec=pltpu.PrefetchScalarGridSpec(
            num_scalar_prefetch=1,
            grid=(1,),
            in_specs=[ANY] * 5,
            out_specs=[pl.BlockSpec((m, 2048), lambda i, p: (0, 0))] * 2,
            scratch_shapes=[pltpu.VMEM((8, m, 256), jnp.bfloat16), pltpu.SemaphoreType.DMA((8,))],
        ),
        out_shape=[jax.ShapeDtypeStruct((m, 2048), jnp.bfloat16)] * 2,
        compiler_params=PARAMS,
        cost_estimate=pl.CostEstimate(flops=0, bytes_accessed=8 * 2 * m * 2048, transcendentals=0),
        name="order_columns",
    )(at, *own, other)


def pick_tiles(at, names, pieces, which):
    _, b, n = pieces[0].shape

    def kernel(at_ref, name_ref, *refs):
        pieces, (out, zeros, sems) = refs[:5], refs[5:]
        spots = [2 * lax.rem(at_ref[X] + (d + 4), 4) + s for d in ORDER for s in range(2)]
        match = [(name_ref[j] // 8 == at_ref[which]).astype(jnp.int32) for j in range(8)]
        slots = []
        for j in range(8):
            before = sum(match[i] * (spots[i] < spots[j]).astype(jnp.int32) for i in range(8) if i != j)
            slots.append(jnp.where(at_ref[CORE] == 1, 1 - before, before))
        for s in range(2):
            there = [match[j] * (slots[j] == s).astype(jnp.int32) for j in range(8)]

            @pl.when(sum(there) == 0)
            def _():
                zeros[...] = jnp.zeros_like(zeros)
                pltpu.make_async_copy(zeros, out.at[s], sems.at[s]).start()

            for j in range(8):

                @pl.when(there[j] == 1)
                def _():
                    source = pieces[j // 2].at[j % 2] if j < 6 else pieces[j - 3].at[0]
                    pltpu.make_async_copy(source, out.at[s], sems.at[s]).start()

        for s in range(2):
            pltpu.make_async_copy(zeros, out.at[s], sems.at[s]).wait()

    return pl.pallas_call(
        kernel,
        grid_spec=pltpu.PrefetchScalarGridSpec(
            num_scalar_prefetch=2,
            grid=(1,),
            in_specs=[ANY] * 5,
            out_specs=ANY,
            scratch_shapes=[pltpu.VMEM((b, n), jnp.bfloat16), pltpu.SemaphoreType.DMA((2,))],
        ),
        out_shape=jax.ShapeDtypeStruct((2, b, n), jnp.bfloat16),
        compiler_params=PARAMS,
        cost_estimate=pl.CostEstimate(flops=0, bytes_accessed=8 * b * n, transcendentals=0),
        name="pick_tiles",
    )(at, names, *pieces)


def merge_tiles(mine, got, cuts):
    _, b, n = mine.shape
    edges = [0, *cuts, n]

    def kernel(mine_ref, got_ref, *outs):
        for out, low, high in zip(outs, edges, edges[1:]):
            out[...] = mine_ref[:, :, low:high] + got_ref[:, :, low:high]

    return pl.pallas_call(
        kernel,
        out_shape=[jax.ShapeDtypeStruct((2, b, v - u), jnp.bfloat16) for u, v in zip(edges, edges[1:])],
        compiler_params=PARAMS,
        cost_estimate=pl.CostEstimate(flops=0, bytes_accessed=12 * b * n, transcendentals=0),
        name="merge_tiles",
    )(mine, got)


def product(left, at, pieces, n, total=None, out=None, column=0, width=None):
    m = left.shape[0]
    step = 512
    depth = sum(p.shape[0] * p.shape[1] for p in pieces)
    first, count = column // step, len(pieces)
    specs = [pl.BlockSpec((m, depth), lambda i: (0, at // depth))]
    specs += [pl.BlockSpec(p.shape[:2] + (step,), lambda i: (0, 0, i)) for p in pieces]
    operands = [left, *pieces]
    if total is not None:
        specs.append(pl.BlockSpec(memory_space=pltpu.VMEM))
        operands.append(total)
    alias = {}
    if out is not None:
        specs.append(ANY)
        alias = {len(operands): 0}
        operands.append(out)

    def kernel(left_ref, *refs):
        result = None if total is None else refs[count][:, pl.ds(pl.multiple_of(pl.program_id(0) * step, step), step)]
        low = 0
        for piece in refs[:count]:
            high = low + piece.shape[0] * piece.shape[1]
            right = piece[...].reshape(high - low, step)
            term = jnp.dot(left_ref[:, low:high], right, preferred_element_type=jnp.float32)
            result = term if result is None else result + term
            low = high
        refs[-1][...] = result.astype(refs[-1].dtype)

    shape = jax.ShapeDtypeStruct((m, n), jnp.float32) if width is None else jax.ShapeDtypeStruct((m, width), jnp.bfloat16)
    return pl.pallas_call(
        kernel,
        grid=(n // step,),
        in_specs=specs,
        out_specs=pl.BlockSpec((m, step), lambda i: (0, first + i)),
        out_shape=shape,
        input_output_aliases=alias,
        compiler_params=PARAMS,
        cost_estimate=pl.CostEstimate(
            flops=2 * WEIGHT * m * depth * n, bytes_accessed=2 * WEIGHT * (m * depth + (depth + 2 * m) * n), transcendentals=0
        ),
        name="product",
    )(*operands)


def per_device(blocks, block_atom, block_pair, atom_sizes, density, density_pattern):
    b, width = blocks.shape[1], blocks.shape[2]
    r, c = lax.axis_index("row"), lax.axis_index("col")
    x, k, z, y = r // 2, r % 2, c // 4, c % 4
    i32 = jnp.int32
    at = jnp.stack([r, r + 1 - 2 * k, x, k, z, y, c]).astype(i32)

    def around(v, shift):
        return [v, shift(v, 1), shift(v, -1), shift(v, 2)]

    def forward(sides, shift):
        first, second = halves(*sides)
        return [shift(first, 1), shift(second, -1)]

    name = (8 * block_pair + jnp.clip(block_atom - 8 * c, 0, 7)).astype(jnp.float32)
    name = jnp.stack(around(jnp.broadcast_to(name, (2, BESIDE)), shift_z))
    near = relay(blocks, shift_row_x, (name,))
    name = jnp.concatenate(around(name, shift_y))
    names = jnp.concatenate(around(name, shift_row_x), axis=1)

    here = names[0, :, 0].astype(i32)
    theirs = swap_core(pick_tiles(at, here, near, OTHER))
    v1, v2 = merge_tiles(pick_tiles(at, here, near, ROW), theirs, [width // 2])
    pieces1, pieces2 = relay(v1, shift_z), relay(v2, shift_y)

    others = swap_core(names)
    chosen = [choose_columns(at, atom_sizes, density, names, others, density_pattern, d) for d in range(4)]
    own = [chosen[0]] + [shift_row_x(chosen[d], d) for d in (1, 2, 3)]

    g1, g2 = join(pieces1), join(pieces2)
    sides1, sides2 = [shift_y(g1, 1), shift_y(g1, -1)], [shift_z(g2, 1), shift_z(g2, -1)]
    last1, last2 = forward(sides1, shift_y), forward(sides2, shift_z)

    other = swap_core(jnp.stack([piece[1] for piece in own]))
    left1, left2 = order_columns(at, own, other)

    half = width // 2
    total1 = product(left1, 0, [g1, *sides1], half)
    total2 = product(left2, 0, [g2, *sides2], half)
    out = product(left1, 24 * b, last1, half, total1, None, 0, width)
    out = product(left2, 24 * b, last2, half, total2, out, half, width)
    return out[None]


def solution(mesh):
    placed = (
        P("row", "col", None),
        P("row", "col"),
        P("row", "col"),
        P(),
        P("col", "row"),
        P("col", "row"),
    )
    return jax.shard_map(
        per_device, mesh=mesh, in_specs=placed, out_specs=P("row", "col", None), check_vma=False
    )
```

```python
import functools

import jax
import jax.numpy as jnp
from jax import lax
from jax.experimental import pallas as pl
from jax.experimental.pallas import tpu as pltpu
from jax.sharding import PartitionSpec as P

ORDER = (0, -1, 1, 2)
VMEM = 14 * 1024 * 1024
BESIDE = 128
WEIGHT = 2
PARAMS = pltpu.CompilerParams(vmem_limit_bytes=VMEM)
ANY = pl.BlockSpec(memory_space=pl.ANY)


def shift_row_x(v, d):
    return lax.ppermute(v, "row", [(2 * x + k, 2 * ((x + d) % 4) + k) for x in range(4) for k in range(2)])


def swap_core(v):
    return lax.ppermute(v, "row", [(r, r ^ 1) for r in range(8)])


def shift_z(v, d):
    return lax.ppermute(v, "col", [(4 * z + y, 4 * ((z + d) % 4) + y) for z in range(4) for y in range(4)])


def shift_y(v, d):
    return lax.ppermute(v, "col", [(4 * z + y, 4 * z + (y + d) % 4) for z in range(4) for y in range(4)])


def copy_parts(inputs, outputs, others=()):
    heights = [sum(high - low for _, low, high in parts) for parts in outputs]
    skip, total = len(inputs) + len(others), sum(len(parts) for parts in outputs)

    def kernel(*refs):
        sems, copies = refs[-1], []
        for parts, out in zip(outputs, refs[skip:]):
            at = 0
            for i, low, high in parts:
                source, target = refs[i].at[pl.ds(low, high - low)], out.at[pl.ds(at, high - low)]
                copies.append(pltpu.make_async_copy(source, target, sems.at[len(copies)]))
                at += high - low
        for copy in copies:
            copy.start()
        for copy in copies:
            copy.wait()

    tail = inputs[0].shape[1:]
    return pl.pallas_call(
        kernel,
        in_specs=[ANY] * skip,
        out_specs=[ANY] * len(outputs),
        out_shape=[jax.ShapeDtypeStruct((h,) + tail, jnp.bfloat16) for h in heights],
        scratch_shapes=[pltpu.SemaphoreType.DMA((total,))],
        compiler_params=PARAMS,
        cost_estimate=pl.CostEstimate(flops=0, bytes_accessed=4 * sum(heights) * tail[0] * tail[1], transcendentals=0),
        name="copy_parts",
    )(*inputs, *others)


def halves(minus, plus, others=()):
    count = minus.shape[0]
    return copy_parts([minus, plus], [[(0, 0, count // 2)], [(1, count // 2, count)]], others)


def relay(v, shift, others=()):
    minus, plus = shift(v, 1), shift(v, -1)
    first, second = halves(minus, plus, others)
    return [v, minus, plus, shift(first, 1), shift(second, -1)]


def join(pieces):
    return copy_parts(pieces, [[(i, 0, p.shape[0]) for i, p in enumerate(pieces)]])[0]


ROW, OTHER, X, CORE, Z, Y, COL = range(7)


def place_of(distance):
    return jnp.where(distance == 0, 0, jnp.where(distance == 3, 1, jnp.where(distance == 1, 2, 3)))


def choose_kernel(d, at_ref, size_ref, density_ref, own_ref, other_ref, pattern_ref, out_ref):
    x, core = at_ref[X], at_ref[CORE]
    pair = 2 * lax.rem(x + d, 4) + lax.rem(core + pl.program_id(0), 2)
    i32 = jnp.int32
    sub = lax.broadcasted_iota(i32, (8, BESIDE), 0)
    lane = lax.broadcasted_iota(i32, (1, BESIDE), 1)
    unit = lax.rem(lane, 64)
    spot = jnp.zeros_like(sub)
    for i, d in enumerate(ORDER):
        spot = jnp.where(sub // 2 == i, 2 * lax.rem(x + (d + 4), 4), spot)
    spot = spot + lax.rem(sub, 2)
    rows, patterns = [], []
    for b in range(2):
        away_y = lax.rem(2 * core + b - at_ref[Y] + 4, 4)
        away_z = lax.rem(x - at_ref[Z] + 4, 4)
        piece = 4 * place_of(away_y) + place_of(away_z)
        own, other = own_ref[piece].astype(i32), other_ref[piece].astype(i32)
        atoms = []
        for names in (jnp.where(core == 0, own, other), jnp.where(core == 0, other, own)):
            match = names // 8 == pair
            low = jnp.min(jnp.where(match, spot, 99), axis=0, keepdims=True)
            high = jnp.max(jnp.where(match, spot, -1), axis=0, keepdims=True)
            atom = names - 8 * pair
            one = jnp.max(jnp.where(match & (spot == low), atom, -1), axis=0, keepdims=True)
            two = jnp.max(jnp.where(match & (spot == high) & (high > low), atom, -1), axis=0, keepdims=True)
            atoms.append((one, two))
        slots = [jnp.where(atoms[j][0] >= 0, atoms[j][0], atoms[1 - j][1]) for j in range(2)]
        atom = jnp.where(lane < 64, slots[0], slots[1])
        size = jnp.zeros_like(atom)
        pattern = jnp.zeros((8, BESIDE), jnp.float32)
        for j in range(8):
            size = jnp.where(atom == j, size_ref[16 * at_ref[ROW] + 8 * b + j], size)
            pattern = jnp.where(atom == j, pattern_ref[:, 8 * b + j : 8 * b + j + 1].astype(jnp.float32), pattern)
        rows.append(jnp.where((atom >= 0) & (unit < size), (8 * b + atom) * 64 + unit, -1))
        patterns.append(pattern)
    rows, pattern = jnp.concatenate(rows, axis=1), jnp.concatenate(patterns, axis=1)
    hit = lax.broadcasted_iota(i32, (density_ref.shape[1], rows.shape[1]), 0) == rows
    picked = jnp.dot(density_ref[...], hit.astype(jnp.bfloat16), preferred_element_type=jnp.float32)
    row = lax.broadcasted_iota(i32, (64, rows.shape[1]), 0)
    for j in range(8):
        factor = jnp.where(row < size_ref[8 * at_ref[COL] + j], pattern[j : j + 1], 0.0)
        out_ref[0, 64 * j : 64 * j + 64] = (picked[64 * j : 64 * j + 64] * factor).astype(jnp.bfloat16)


def choose_columns(at, sizes, density, own, other, pattern, d):
    m, width = density.shape
    names = pl.BlockSpec(own.shape, lambda t, p, q: (0, 0, 0))
    return pl.pallas_call(
        functools.partial(choose_kernel, d),
        grid_spec=pltpu.PrefetchScalarGridSpec(
            num_scalar_prefetch=2,
            grid=(2,),
            in_specs=[
                pl.BlockSpec((m, width), lambda t, p, q: (0, 0)),
                names,
                names,
                pl.BlockSpec(pattern.shape, lambda t, p, q: (0, 0)),
            ],
            out_specs=pl.BlockSpec((1, m, 256), lambda t, p, q: (t, 0, 0)),
        ),
        out_shape=jax.ShapeDtypeStruct((2, m, 256), jnp.bfloat16),
        compiler_params=PARAMS,
        cost_estimate=pl.CostEstimate(flops=2 * m * width * 512, bytes_accessed=2 * m * (width + 512), transcendentals=0),
        name="choose_columns",
    )(at, sizes, density, own, other, pattern)


def order_kernel(at_ref, *refs):
    own, other, (left1, left2), (blocks, sems) = refs[:4], refs[4], refs[5:7], refs[7:]
    copies = [pltpu.make_async_copy(own[d].at[0], blocks.at[d], sems.at[d]) for d in range(4)]
    copies += [pltpu.make_async_copy(other.at[d], blocks.at[4 + d], sems.at[4 + d]) for d in range(4)]
    for copy in copies:
        copy.start()
    for copy in copies:
        copy.wait()
    for i in range(16):
        j = (i % 4) * 4 + i // 4
        from_y = lax.rem(at_ref[Y] + (ORDER[i // 4] + 4), 4)
        from_z = lax.rem(at_ref[Z] + (ORDER[i % 4] + 4), 4)
        place = lax.rem(at_ref[X] - from_z + 4, 4) + jnp.where(from_y // 2 == at_ref[CORE], 0, 4)
        block = blocks[place, :, pl.ds(pl.multiple_of(lax.rem(from_y, 2) * 128, 128), 128)]
        left1[:, i * 128 : (i + 1) * 128] = block
        left2[:, j * 128 : (j + 1) * 128] = block


def order_columns(at, own, other):
    m = other.shape[1]
    return pl.pallas_call(
        order_kernel,
        grid_spec=pltpu.PrefetchScalarGridSpec(
            num_scalar_prefetch=1,
            grid=(1,),
            in_specs=[ANY] * 5,
            out_specs=[pl.BlockSpec((m, 2048), lambda i, p: (0, 0))] * 2,
            scratch_shapes=[pltpu.VMEM((8, m, 256), jnp.bfloat16), pltpu.SemaphoreType.DMA((8,))],
        ),
        out_shape=[jax.ShapeDtypeStruct((m, 2048), jnp.bfloat16)] * 2,
        compiler_params=PARAMS,
        cost_estimate=pl.CostEstimate(flops=0, bytes_accessed=8 * 2 * m * 2048, transcendentals=0),
        name="order_columns",
    )(at, *own, other)


def pick_tiles(at, names, pieces, which):
    _, b, n = pieces[0].shape

    def kernel(at_ref, name_ref, *refs):
        pieces, (out, zeros, sems) = refs[:5], refs[5:]
        spots = [2 * lax.rem(at_ref[X] + (d + 4), 4) + s for d in ORDER for s in range(2)]
        match = [(name_ref[j] // 8 == at_ref[which]).astype(jnp.int32) for j in range(8)]
        slots = []
        for j in range(8):
            before = sum(match[i] * (spots[i] < spots[j]).astype(jnp.int32) for i in range(8) if i != j)
            slots.append(jnp.where(at_ref[CORE] == 1, 1 - before, before))
        for s in range(2):
            there = [match[j] * (slots[j] == s).astype(jnp.int32) for j in range(8)]

            @pl.when(sum(there) == 0)
            def _():
                zeros[...] = jnp.zeros_like(zeros)
                pltpu.make_async_copy(zeros, out.at[s], sems.at[s]).start()

            for j in range(8):

                @pl.when(there[j] == 1)
                def _():
                    source = pieces[j // 2].at[j % 2] if j < 6 else pieces[j - 3].at[0]
                    pltpu.make_async_copy(source, out.at[s], sems.at[s]).start()

        for s in range(2):
            pltpu.make_async_copy(zeros, out.at[s], sems.at[s]).wait()

    return pl.pallas_call(
        kernel,
        grid_spec=pltpu.PrefetchScalarGridSpec(
            num_scalar_prefetch=2,
            grid=(1,),
            in_specs=[ANY] * 5,
            out_specs=ANY,
            scratch_shapes=[pltpu.VMEM((b, n), jnp.bfloat16), pltpu.SemaphoreType.DMA((2,))],
        ),
        out_shape=jax.ShapeDtypeStruct((2, b, n), jnp.bfloat16),
        compiler_params=PARAMS,
        cost_estimate=pl.CostEstimate(flops=0, bytes_accessed=8 * b * n, transcendentals=0),
        name="pick_tiles",
    )(at, names, *pieces)


def merge_tiles(mine, got, cuts):
    _, b, n = mine.shape
    edges = [0, *cuts, n]

    def kernel(mine_ref, got_ref, *outs):
        for out, low, high in zip(outs, edges, edges[1:]):
            out[...] = mine_ref[:, :, low:high] + got_ref[:, :, low:high]

    return pl.pallas_call(
        kernel,
        out_shape=[jax.ShapeDtypeStruct((2, b, v - u), jnp.bfloat16) for u, v in zip(edges, edges[1:])],
        compiler_params=PARAMS,
        cost_estimate=pl.CostEstimate(flops=0, bytes_accessed=12 * b * n, transcendentals=0),
        name="merge_tiles",
    )(mine, got)


def product(left, at, pieces, n, total=None, out=None, column=0, width=None):
    m = left.shape[0]
    step = 512
    depth = sum(p.shape[0] * p.shape[1] for p in pieces)
    first, count = column // step, len(pieces)
    specs = [pl.BlockSpec((m, depth), lambda i: (0, at // depth))]
    specs += [pl.BlockSpec(p.shape[:2] + (step,), lambda i: (0, 0, i)) for p in pieces]
    operands = [left, *pieces]
    if total is not None:
        specs.append(pl.BlockSpec(memory_space=pltpu.VMEM))
        operands.append(total)
    alias = {}
    if out is not None:
        specs.append(ANY)
        alias = {len(operands): 0}
        operands.append(out)

    def kernel(left_ref, *refs):
        result = None if total is None else refs[count][:, pl.ds(pl.multiple_of(pl.program_id(0) * step, step), step)]
        low = 0
        for piece in refs[:count]:
            high = low + piece.shape[0] * piece.shape[1]
            right = piece[...].reshape(high - low, step)
            term = jnp.dot(left_ref[:, low:high], right, preferred_element_type=jnp.float32)
            result = term if result is None else result + term
            low = high
        refs[-1][...] = result.astype(refs[-1].dtype)

    shape = jax.ShapeDtypeStruct((m, n), jnp.float32) if width is None else jax.ShapeDtypeStruct((m, width), jnp.bfloat16)
    return pl.pallas_call(
        kernel,
        grid=(n // step,),
        in_specs=specs,
        out_specs=pl.BlockSpec((m, step), lambda i: (0, first + i)),
        out_shape=shape,
        input_output_aliases=alias,
        compiler_params=PARAMS,
        cost_estimate=pl.CostEstimate(
            flops=2 * WEIGHT * m * depth * n, bytes_accessed=2 * WEIGHT * (m * depth + (depth + 2 * m) * n), transcendentals=0
        ),
        name="product",
    )(*operands)


def per_device(blocks, block_atom, block_pair, atom_sizes, density, density_pattern):
    b, width = blocks.shape[1], blocks.shape[2]
    r, c = lax.axis_index("row"), lax.axis_index("col")
    x, k, z, y = r // 2, r % 2, c // 4, c % 4
    i32 = jnp.int32
    at = jnp.stack([r, r + 1 - 2 * k, x, k, z, y, c]).astype(i32)

    def around(v, shift):
        return [v, shift(v, 1), shift(v, -1), shift(v, 2)]

    def forward(sides, shift):
        first, second = halves(*sides)
        return [shift(first, 1), shift(second, -1)]

    name = (8 * block_pair + jnp.clip(block_atom - 8 * c, 0, 7)).astype(jnp.float32)
    name = jnp.stack(around(jnp.broadcast_to(name, (2, BESIDE)), shift_z))
    near = relay(blocks, shift_row_x, (name,))
    name = jnp.concatenate(around(name, shift_y))
    names = jnp.concatenate(around(name, shift_row_x), axis=1)

    here = names[0, :, 0].astype(i32)
    theirs = swap_core(pick_tiles(at, here, near, OTHER))
    v1, v2 = merge_tiles(pick_tiles(at, here, near, ROW), theirs, [width // 2])
    pieces1, pieces2 = relay(v1, shift_z), relay(v2, shift_y)

    others = swap_core(names)
    chosen = [choose_columns(at, atom_sizes, density, names, others, density_pattern, d) for d in range(4)]
    own = [chosen[0]] + [shift_row_x(chosen[d], d) for d in (1, 2, 3)]

    g1, g2 = join(pieces1), join(pieces2)
    sides1, sides2 = [shift_y(g1, 1), shift_y(g1, -1)], [shift_z(g2, 1), shift_z(g2, -1)]
    last1, last2 = forward(sides1, shift_y), forward(sides2, shift_z)

    other = swap_core(jnp.stack([piece[1] for piece in own]))
    left1, left2 = order_columns(at, own, other)

    half = width // 2
    total1 = product(left1, 0, [g1, *sides1], half)
    total2 = product(left2, 0, [g2, *sides2], half)
    out = product(left1, 24 * b, last1, half, total1, None, 0, width)
    out = product(left2, 24 * b, last2, half, total2, out, half, width)
    return out[None]


def solution(mesh):
    placed = (
        P("row", "col", None),
        P("row", "col"),
        P("row", "col"),
        P(),
        P("col", "row"),
        P("col", "row"),
    )
    return jax.shard_map(
        per_device, mesh=mesh, in_specs=placed, out_specs=P("row", "col", None), check_vma=False
    )
```
